32 devices in a mesh: groups: 2 (over y), enrol: 4 (over z), probe: 4 (over x, core).
Axes of the slice: x: 2, y: 2, z: 4, core: 2. Of those that a mesh axis runs over, the one named last changes fastest.
Arguments:
- images: float32 [16384, 512], P(('groups', 'enrol', 'probe')), parts along dimension 0, may hold values from -6 to 6
- w_first: float32 [512, 2048], replicated, may hold values from -0.25 to 0.25
- w_second: float32 [2048, 256], replicated, may hold values from -0.125 to 0.125
- calib_scale: float32 [1], replicated, may hold values from 5 to 20
- calib_bias: float32 [1], replicated, may hold values from -2 to 2
- template_slot: int32 [16384], P(('groups', 'enrol', 'probe')), parts along dimension 0, may hold values from 0 to 191
- media_counts: int32 [32, 16], P(('groups', 'enrol', 'probe')), parts along dimension 0, may hold values from 1 to 64, as said below
Outputs:
- scores: bfloat16 [4096, 1024], P(('groups', 'enrol'), 'probe'), parts along dimension 0
The draws below stay inside these ranges and needn't reach their ends.
There are 2 independent parts, one for each index of `groups`. The reference program is written for one: setup_inputs(seed, part) draws one part's arguments, and reference() takes and returns one part's arrays. A program takes and returns all parts, laid end to end along the dimension named above; an argument that names none is the same for every part. Nothing has to cross between parts.
Inputs may be any that keep to these rules, and one draw needn't show every extreme that they name: `media_counts`: each row sums to 512; in every draw one owner receives exactly 64 images from every device.
All inputs are finite; a program needn't handle non-finite values.
Results may differ from the reference program's by a relative error of at most 0.001.
Values sent between devices are 32-bit elements; how exact they have to be, the bound alone decides.
A program may use at most 64 MiB of HBM per device.

```python
import math
import jax
import jax.numpy as jnp
from jax import lax

D_IN = 512
HIDDEN_SIZE = 2048
D_EMB = 256
IMG_DEV = 512
ET_OWN = 128
PT_OWN = 64
SLOTS = 192
IMAGES = 8192
ENROL = 2048
PROBE = 1024
N_ENROL = 4
N_PROBE = 4


def draw_media_counts(key, part):
    owners = N_ENROL * N_PROBE
    capacity = 2 * IMG_DEV // owners
    others = owners - 1
    per_owner = capacity - 1
    tickets = others * per_owner
    extra = IMG_DEV - capacity - others
    hot_owner = jax.random.randint(jax.random.fold_in(key, 7), (), 0, owners)
    owner_ids = jnp.arange(owners, dtype=jnp.int32)
    other_ids = jnp.arange(others, dtype=jnp.int32)
    rest_index = owner_ids - (owner_ids > hot_owner).astype(jnp.int32)
    rest_index = jnp.clip(rest_index, 0, others - 1)

    def one_row(row):
        row_key = jax.random.fold_in(jax.random.fold_in(key, 11), row)
        shuffled = jax.random.permutation(row_key, tickets).astype(jnp.int32)
        taken = jnp.arange(tickets, dtype=jnp.int32) < extra
        holder = shuffled // per_owner
        hits = (holder[:, None] == other_ids[None, :]) & taken[:, None]
        rest_counts = 1 + jnp.sum(hits.astype(jnp.int32), axis=0)
        counts = jnp.where(owner_ids == hot_owner, capacity, rest_counts[rest_index])
        return counts.astype(jnp.int32)
    return jax.vmap(one_row)(jnp.arange(owners, dtype=jnp.int32))


def plant(array, stream_key, least, largest):
    longest = array.shape.index(max(array.shape))
    spots = []
    for shift in (0, 1):
        where = [jax.random.randint(jax.random.fold_in(stream_key, axis), (), 0, length) for axis, length in enumerate(array.shape)]
        where[longest] = (where[longest] + shift) % array.shape[longest]
        spots.append(tuple(where))
    return array.at[spots[0]].set(least).at[spots[1]].set(largest)


def block_scale(stream_key, dims, pieces, low, largest):
    def one(dim, shards_of):
        heights = jax.random.uniform(jax.random.fold_in(jax.random.fold_in(stream_key, 6), dim), (shards_of,), jnp.float32, low / len(pieces), largest / len(pieces))
        return jnp.repeat(jnp.exp(heights), dims[dim] // shards_of).reshape((-1,) + (1,) * (len(dims) - dim - 1))

    gain = one(*pieces[0])
    for cut in pieces[1:]:
        gain = gain * one(*cut)
    return gain


def bell_draw(rng, dims, scale, bound, split=(), kind=jnp.bfloat16):
    loudness = block_scale(rng, dims, split, -0.22, 0.18) if split else 1.0
    array = jax.random.normal(rng, dims, jnp.float32) * scale * loudness
    return jnp.minimum(jnp.maximum(array, -bound), bound).astype(kind)


def setup_inputs(seed: int = 0, part: int = 0) -> dict:
    arg_keys = jax.random.split(jax.random.key(seed), 8)
    part_splits = jax.random.split(jax.random.fold_in(arg_keys[7], part), 8)
    images = bell_draw(part_splits[0], (IMAGES, D_IN), 1.0, 6.0, ((0, 16),), jnp.float32)
    w_first = bell_draw(arg_keys[1], (D_IN, HIDDEN_SIZE), D_IN ** -0.5, 0.25, (), jnp.float32)
    w_second = bell_draw(arg_keys[2], (HIDDEN_SIZE, D_EMB), HIDDEN_SIZE ** -0.5, 0.125, (), jnp.float32)
    calib_scale = jnp.clip(jnp.exp(jax.random.uniform(arg_keys[3], (1,), jnp.float32, math.log(5.0), math.log(20.0))), 5.0, 20.0)
    calib_bias = jnp.clip(jax.random.uniform(arg_keys[4], (1,), jnp.float32, -2.0, 2.0), -2.0, 2.0)
    template_slot = plant(jax.random.randint(part_splits[5], (IMAGES,), 0, SLOTS), jax.random.fold_in(part_splits[5], 1), 0, SLOTS - 1).astype(jnp.int32)
    media_counts = draw_media_counts(jax.random.fold_in(jax.random.fold_in(arg_keys[7], part), 71), part)
    return dict(images=images, w_first=w_first, w_second=w_second, calib_scale=calib_scale, calib_bias=calib_bias, template_slot=template_slot, media_counts=media_counts)


HIGH = lax.Precision.HIGHEST

def unit_rows(table):
    return table * lax.rsqrt(lax.optimization_barrier(jnp.sum(table * table, axis=-1, keepdims=True)) + 1e-06)

def reference(images, w_first, w_second, calib_scale, calib_bias, template_slot, media_counts):
    owners = N_ENROL * N_PROBE
    blocks = images.reshape(owners, IMG_DEV, D_IN)

    def embed_block(block):
        hidden = jax.nn.gelu(jnp.dot(block, w_first, precision=HIGH, preferred_element_type=jnp.float32))
        feature = jnp.dot(hidden, w_second, precision=HIGH, preferred_element_type=jnp.float32)
        return unit_rows(feature)
    embedding = lax.map(embed_block, blocks).reshape(IMAGES, D_EMB)
    ends = jnp.cumsum(media_counts, axis=1).astype(jnp.int32)
    position = jnp.arange(IMG_DEV, dtype=jnp.int32)
    owner = lax.optimization_barrier(jnp.sum((ends[:, None, :] <= position[None, :, None]).astype(jnp.int32), axis=2)).reshape(IMAGES)
    owner = owner.astype(jnp.int32)
    slot = template_slot.astype(jnp.int32)
    erow = owner // N_PROBE
    pcol = owner % N_PROBE
    is_enrol = slot < ET_OWN
    enrol_index = jnp.where(is_enrol, owner * ET_OWN + slot, ENROL).astype(jnp.int32)
    probe_index = jnp.where(is_enrol, PROBE, pcol * (N_ENROL * PT_OWN) + erow * PT_OWN + slot - ET_OWN).astype(jnp.int32)
    enrol_sum = jax.ops.segment_sum(embedding, enrol_index, num_segments=ENROL + 1)[:ENROL]
    probe_sum = jax.ops.segment_sum(embedding, probe_index, num_segments=PROBE + 1)[:PROBE]
    enrol_unit = unit_rows(enrol_sum)
    probe_unit = unit_rows(probe_sum)
    cosine = jnp.dot(enrol_unit, probe_unit.T, precision=HIGH, preferred_element_type=jnp.float32)
    return jax.nn.sigmoid(calib_scale[0] * cosine + calib_bias[0]).astype(jnp.bfloat16)
```

```python
import functools

import jax
import jax.numpy as jnp
from jax import lax
from jax.experimental import pallas as pl
from jax.experimental.pallas import tpu as pltpu
from jax.sharding import PartitionSpec as P

ET_OWN = 128
PT_OWN = 64
LANES = 128
MESH = pl.DeviceIdType.MESH
F32 = jnp.float32
BF16 = jnp.bfloat16


def split(x):
    high = x.astype(BF16)
    return high, (x - high.astype(F32)).astype(BF16)


def one_hot(mask):
    return jnp.where(mask, 1.0, 0.0).astype(BF16)


def nt(a, b):
    return lax.dot_general(a, b, (((1,), (1,)), ((), ())), preferred_element_type=F32)


def kernel(
    ne, np_, chunk,
    images, w_first, w_second, scale, bias, slots, counts,
    out,
    w1, w2, gather, catted, slot_tiles, slot_send, slot_recv, send, recv, pool, enrol, probe,
    w1_sem, w2_sem, ss_sem, sr_sem, rs_sem, rr_sem, es_sem, er_sem, ps_sem, pr_sem,
):
    n = ne * np_
    images_here = images.shape[0]
    cap = 2 * images_here // n
    total = n * cap
    width = w_second.shape[1]
    g, e, p = lax.axis_index("groups"), lax.axis_index("enrol"), lax.axis_index("probe")
    me = e * np_ + p

    def device(o):
        return (g, o // np_, lax.rem(o, np_))

    barrier = pltpu.get_barrier_semaphore()

    def greet(k, c):
        pl.semaphore_signal(
            barrier, inc=1, device_id=device(lax.rem(me + k, n)), device_id_type=MESH
        )
        return c

    lax.fori_loop(1, n, greet, 0)

    chunks = w1.shape[0]
    loads = []
    for c in range(chunks):
        a = pltpu.make_async_copy(w_first.at[:, pl.ds(c * chunk, chunk)], w1.at[c], w1_sem.at[c])
        b = pltpu.make_async_copy(w_second.at[pl.ds(c * chunk, chunk), :], w2.at[c], w2_sem.at[c])
        a.start()
        b.start()
        loads.append((a, b))

    at = lax.broadcasted_iota(jnp.int32, (1, images_here), 1)

    def place(k, carry):
        dest, end = carry
        end = end + counts[0, k]
        return dest + jnp.where(at >= end, cap - counts[0, k], 0), end

    dest, _ = lax.fori_loop(0, n, place, (at, jnp.int32(0)), unroll=n <= 16)
    rows = lax.broadcasted_iota(jnp.int32, (LANES, images_here), 0)
    wanted = jnp.broadcast_to((slots[...] + 1).astype(F32), (8, images_here)).astype(BF16)
    for j in range(total // LANES):
        tile = one_hot(rows + j * LANES == dest)
        gather[pl.ds(j * LANES, LANES), :] = tile
        slot_tiles[j] = nt(wanted, tile)

    pl.semaphore_wait(barrier, n - 1)

    my_off = lax.rem(me * cap, LANES)
    lane = lax.broadcasted_iota(jnp.int32, (8, LANES), 1)
    mine = (lane >= my_off) & (lane < my_off + cap)

    def slot_row(o):
        tile = slot_tiles[(o * cap) // LANES]
        shift = lax.rem(my_off - lax.rem(o * cap, LANES) + LANES, LANES)
        return jnp.where(mine, pltpu.roll(tile, shift, 1), 0.0)

    def slot_copy(o, source):
        return pltpu.make_async_remote_copy(
            src_ref=slot_send.at[o], dst_ref=slot_recv.at[source],
            send_sem=ss_sem.at[o], recv_sem=sr_sem.at[source],
            device_id=device(o), device_id_type=MESH,
        )

    def row_copy(o, source):
        return pltpu.make_async_remote_copy(
            src_ref=send.at[o], dst_ref=recv.at[source],
            send_sem=rs_sem.at[o], recv_sem=rr_sem.at[source],
            device_id=device(o), device_id_type=MESH,
        )

    def send_slots(k, c):
        o = lax.rem(me + k, n)
        slot_send[o] = slot_row(o)
        slot_copy(o, me).start()
        return c

    lax.fori_loop(1, n, send_slots, 0)
    slot_recv[me] = slot_row(me)

    xh, xl = split(images[...])
    x3 = jnp.concatenate([xh, xl, xh], axis=1)
    feature = None
    for c in range(chunks):
        loads[c][0].wait()
        ah, al = split(w1[c])
        hidden = jax.nn.gelu(
            jnp.dot(x3, jnp.concatenate([ah, ah, al], axis=0), preferred_element_type=F32)
        )
        hh, hl = split(hidden)
        loads[c][1].wait()
        bh, bl = split(w2[c])
        part = jnp.dot(
            jnp.concatenate([hh, hl, hh], axis=1),
            jnp.concatenate([bh, bh, bl], axis=0),
            preferred_element_type=F32,
        )
        feature = part if feature is None else feature + part
    embedding = feature * lax.rsqrt(jnp.sum(feature * feature, axis=-1, keepdims=True) + 1e-06)
    h, l = split(embedding)
    catted[:, :width] = h
    catted[:, width:] = l

    half = ne // 2
    here = e // half
    per_row = np_ * cap
    for t in range(ne):
        if t < half:
            er = (1 - here) * half + lax.rem(e + t, half)
        else:
            er = here * half + lax.rem(e + 1 + t - half, half)
        picked = jnp.dot(
            gather[pl.ds(pl.multiple_of(er * per_row, per_row), per_row), :],
            catted[...],
            preferred_element_type=F32,
        )
        picked = (picked[:, :width] + picked[:, width:]).reshape(np_, cap, width)
        send[pl.ds(er * np_, np_)] = picked
        if t < ne - 1:
            for k in range(np_):
                row_copy(er * np_ + lax.rem(p + k, np_), me).start()
        else:
            for k in range(1, np_):
                row_copy(er * np_ + lax.rem(p + k, np_), me).start()
            recv[me] = send[me]

    def slots_in(k, c):
        o = lax.rem(me + k, n)
        slot_copy(o, o).wait_recv()
        return c

    lax.fori_loop(1, n, slots_in, 0)
    owned = pool.shape[0]
    ids = lax.broadcasted_iota(jnp.int32, (owned, LANES), 0) + 1
    together = LANES // cap
    for j in range(total // LANES):
        tile = slot_recv[j * together]
        for k in range(1, together):
            tile = tile + slot_recv[j * together + k]
        pool[:, j * LANES:(j + 1) * LANES] = one_hot(tile[0:1].astype(jnp.int32) == ids)

    def rows_in(k, c):
        o = lax.rem(me + k, n)
        row_copy(o, o).wait_recv()
        return c

    lax.fori_loop(1, n, rows_in, 0)
    h, l = split(recv[...].reshape(total, width))
    pooled = jnp.dot(pool[...], jnp.concatenate([h, l], axis=1), preferred_element_type=F32)
    pooled = pooled[:, :width] + pooled[:, width:]
    templates = pooled * lax.rsqrt(jnp.sum(pooled * pooled, axis=-1, keepdims=True) + 1e-06)
    enrol[p] = templates[:ET_OWN]
    probe[e] = templates[ET_OWN:]

    def enrol_copy(k):
        to = lax.rem(p + k, np_)
        return to, pltpu.make_async_remote_copy(
            src_ref=enrol.at[p], dst_ref=enrol.at[p],
            send_sem=es_sem.at[to], recv_sem=er_sem.at[p],
            device_id=(g, e, to), device_id_type=MESH,
        )

    def enrol_arrival(o):
        return pltpu.make_async_remote_copy(
            src_ref=enrol.at[o], dst_ref=enrol.at[o],
            send_sem=es_sem.at[o], recv_sem=er_sem.at[o],
            device_id=(g, e, o), device_id_type=MESH,
        )

    def probe_copy(to, source):
        return pltpu.make_async_remote_copy(
            src_ref=probe.at[source], dst_ref=probe.at[source],
            send_sem=ps_sem.at[to], recv_sem=pr_sem.at[source],
            device_id=(g, to, p), device_id_type=MESH,
        )

    for k in range(ne - 1, 0, -1):
        probe_copy(lax.rem(e + k, ne), e).start()
    for k in range(np_ - 1, 0, -1):
        enrol_copy(k)[1].start()
    for k in range(1, ne):
        o = lax.rem(e + k, ne)
        probe_copy(o, o).wait_recv()
    for k in range(1, np_):
        enrol_arrival(lax.rem(p + k, np_)).wait_recv()

    ph, pl_ = split(probe[...].reshape(ne * PT_OWN, width))
    right = jnp.concatenate([ph, ph, pl_], axis=1)
    slope, offset = scale[0], bias[0]
    for k in range(np_):
        eh, el = split(enrol[k])
        cosine = nt(jnp.concatenate([eh, el, eh], axis=1), right)
        out[k * ET_OWN:(k + 1) * ET_OWN, :] = jax.nn.sigmoid(slope * cosine + offset).astype(BF16)

    def drain(k, c):
        o = lax.rem(me + k, n)
        slot_copy(o, me).wait_send()
        row_copy(o, me).wait_send()
        return c

    lax.fori_loop(1, n, drain, 0)
    for k in range(1, ne):
        probe_copy(lax.rem(e + k, ne), e).wait_send()
    for k in range(1, np_):
        enrol_copy(k)[1].wait_send()


def shards(ne, np_, images, w_first, w_second, calib_scale, calib_bias, template_slot, media_counts):
    n = ne * np_
    here, features = images.shape
    hidden, width = w_second.shape
    cap = 2 * here // n
    total = n * cap
    chunk = 256
    chunks = hidden // chunk
    vmem = pl.BlockSpec(memory_space=pltpu.VMEM)
    smem = pl.BlockSpec(memory_space=pltpu.SMEM)
    anywhere = pl.BlockSpec(memory_space=pl.ANY)
    dma = pltpu.SemaphoreType.DMA
    return pl.pallas_call(
        functools.partial(kernel, ne, np_, chunk),
        out_shape=jax.ShapeDtypeStruct((np_ * ET_OWN, ne * PT_OWN), BF16),
        in_specs=[vmem, anywhere, anywhere, smem, smem, vmem, smem],
        out_specs=vmem,
        scratch_shapes=[
            pltpu.VMEM((chunks, features, chunk), F32),
            pltpu.VMEM((chunks, chunk, width), F32),
            pltpu.VMEM((total, here), BF16),
            pltpu.VMEM((here, 2 * width), BF16),
            pltpu.VMEM((total // LANES, 8, LANES), F32),
            pltpu.VMEM((n, 8, LANES), F32),
            pltpu.VMEM((n, 8, LANES), F32),
            pltpu.VMEM((n, cap, width), F32),
            pltpu.VMEM((n, cap, width), F32),
            pltpu.VMEM((ET_OWN + PT_OWN, total), BF16),
            pltpu.VMEM((np_, ET_OWN, width), F32),
            pltpu.VMEM((ne, PT_OWN, width), F32),
            dma((chunks,)), dma((chunks,)),
            dma((n,)), dma((n,)), dma((n,)), dma((n,)),
            dma((np_,)), dma((np_,)), dma((ne,)), dma((ne,)),
        ],
        compiler_params=pltpu.CompilerParams(
            collective_id=0, has_side_effects=True, vmem_limit_bytes=50 * 1024 * 1024
        ),
    )(
        images, w_first, w_second, calib_scale, calib_bias,
        template_slot.reshape(1, here), media_counts,
    )


def solution(mesh):
    ne, np_ = mesh.shape["enrol"], mesh.shape["probe"]
    return jax.shard_map(
        functools.partial(shards, ne, np_),
        mesh=mesh,
        in_specs=(
            P(("groups", "enrol", "probe"), None),
            P(),
            P(),
            P(),
            P(),
            P(("groups", "enrol", "probe")),
            P(("groups", "enrol", "probe"), None),
        ),
        out_specs=P(("groups", "enrol"), "probe"),
        check_vma=False,
    )
```

```python
import functools

import jax
import jax.numpy as jnp
from jax import lax
from jax.experimental import pallas as pl
from jax.experimental.pallas import tpu as pltpu
from jax.sharding import PartitionSpec as P

ET_OWN = 128
PT_OWN = 64
LANES = 128
MESH = pl.DeviceIdType.MESH
F32 = jnp.float32
BF16 = jnp.bfloat16


def split(x):
    high = x.astype(BF16)
    return high, (x - high.astype(F32)).astype(BF16)


def one_hot(mask):
    return jnp.where(mask, 1.0, 0.0).astype(BF16)


def nt(a, b):
    return lax.dot_general(a, b, (((1,), (1,)), ((), ())), preferred_element_type=F32)


def kernel(
    ne, np_, chunk,
    images, w_first, w_second, scale, bias, slots, counts,
    out,
    held, w1, w2, w1h, w1l, w2h, w2l, gather, catted, slot_tiles, slot_send, slot_recv, send, recv, pool, enrol, probe,
    x_sem, w1_sem, w2_sem, ss_sem, sr_sem, rs_sem, rr_sem, es_sem, er_sem, ps_sem, pr_sem,
):
    n = ne * np_
    images_here = images.shape[0]
    cap = 2 * images_here // n
    total = n * cap
    width = w_second.shape[1]
    g, e, p = lax.axis_index("groups"), lax.axis_index("enrol"), lax.axis_index("probe")
    me = e * np_ + p

    def device(o):
        return (g, o // np_, lax.rem(o, np_))

    barrier = pltpu.get_barrier_semaphore()

    def greet(k, c):
        pl.semaphore_signal(
            barrier, inc=1, device_id=device(lax.rem(me + k, n)), device_id_type=MESH
        )
        return c

    lax.fori_loop(1, n, greet, 0)

    chunks = w1.shape[0]
    loads = []
    half_rows = images_here // 2
    half = ne // 2
    here = e // half
    pictures = []
    for t in range(2):
        spot = pl.ds(pl.multiple_of((here if t else 1 - here) * half_rows, half_rows), half_rows)
        a = pltpu.make_async_copy(images.at[spot, :], held.at[t], x_sem.at[t])
        a.start()
        pictures.append((spot, a))
    for c in range(chunks):
        a = pltpu.make_async_copy(w_first.at[:, pl.ds(c * chunk, chunk)], w1.at[c], w1_sem.at[c])
        b = pltpu.make_async_copy(w_second.at[pl.ds(c * chunk, chunk), :], w2.at[c], w2_sem.at[c])
        a.start()
        b.start()
        loads.append((a, b))

    at = lax.broadcasted_iota(jnp.int32, (1, images_here), 1)

    def place(k, carry):
        dest, end = carry
        end = end + counts[0, k]
        return dest + jnp.where(at >= end, cap - counts[0, k], 0), end

    dest, _ = lax.fori_loop(0, n, place, (at, jnp.int32(0)), unroll=n <= 16)
    rows = lax.broadcasted_iota(jnp.int32, (LANES, images_here), 0)
    wanted = jnp.broadcast_to((slots[...] + 1).astype(F32), (8, images_here)).astype(BF16)
    for j in range(total // LANES):
        tile = one_hot(rows + j * LANES == dest)
        gather[pl.ds(j * LANES, LANES), :] = tile
        slot_tiles[j] = nt(wanted, tile)

    pl.semaphore_wait(barrier, n - 1)

    my_off = lax.rem(me * cap, LANES)
    lane = lax.broadcasted_iota(jnp.int32, (8, LANES), 1)
    mine = (lane >= my_off) & (lane < my_off + cap)

    def slot_row(o):
        tile = slot_tiles[(o * cap) // LANES]
        shift = lax.rem(my_off - lax.rem(o * cap, LANES) + LANES, LANES)
        return jnp.where(mine, pltpu.roll(tile, shift, 1), 0.0)

    def slot_copy(o, source):
        return pltpu.make_async_remote_copy(
            src_ref=slot_send.at[o], dst_ref=slot_recv.at[source],
            send_sem=ss_sem.at[o], recv_sem=sr_sem.at[source],
            device_id=device(o), device_id_type=MESH,
        )

    def row_copy(o, source):
        return pltpu.make_async_remote_copy(
            src_ref=send.at[o], dst_ref=recv.at[source],
            send_sem=rs_sem.at[o], recv_sem=rr_sem.at[source],
            device_id=device(o), device_id_type=MESH,
        )

    def send_slots(k, c):
        o = lax.rem(me + k, n)
        slot_send[o] = slot_row(o)
        slot_copy(o, me).start()
        return c

    lax.fori_loop(1, n, send_slots, 0)
    slot_recv[me] = slot_row(me)

    per_row = np_ * cap
    early = ne // 4

    def send_row(t, spot):
        if t < half:
            er = (1 - here) * (ne - 1 - t) + here * t
        else:
            er = here * half + lax.rem(e + 1 + t - half, half)
        span = pl.ds(pl.multiple_of(er * per_row, per_row), per_row)
        if spot is None:
            picked = jnp.dot(gather[span, :], catted[...], preferred_element_type=F32)
        else:
            picked = jnp.dot(gather[span, spot], catted[spot, :], preferred_element_type=F32)
        picked = (picked[:, :width] + picked[:, width:]).reshape(np_, cap, width)
        send[pl.ds(er * np_, np_)] = picked
        if t < ne - 1:
            for k in range(np_):
                row_copy(er * np_ + lax.rem(p + k, np_), me).start()
        else:
            for k in range(1, np_):
                row_copy(er * np_ + lax.rem(p + k, np_), me).start()
            recv[me] = send[me]

    for t in range(2):
        spot, arrival = pictures[t]
        arrival.wait()
        xh, xl = split(held[t])
        x3 = jnp.concatenate([xh, xl, xh], axis=1)
        feature = None
        for c in range(chunks):
            if t == 0:
                loads[c][0].wait()
                ah, al = split(w1[c])
                w1h[c], w1l[c] = ah, al
            else:
                ah, al = w1h[c], w1l[c]
            hidden = jax.nn.gelu(
                jnp.dot(x3, jnp.concatenate([ah, ah, al], axis=0), preferred_element_type=F32)
            )
            hh, hl = split(hidden)
            if t == 0:
                loads[c][1].wait()
                bh, bl = split(w2[c])
                w2h[c], w2l[c] = bh, bl
            else:
                bh, bl = w2h[c], w2l[c]
            part = jnp.dot(
                jnp.concatenate([hh, hl, hh], axis=1),
                jnp.concatenate([bh, bh, bl], axis=0),
                preferred_element_type=F32,
            )
            feature = part if feature is None else feature + part
        embedding = feature * lax.rsqrt(jnp.sum(feature * feature, axis=-1, keepdims=True) + 1e-06)
        h, l = split(embedding)
        catted[spot, :] = jnp.concatenate([h, l], axis=1)
        for u in range(early) if t == 0 else range(early, ne):
            send_row(u, spot if t == 0 else None)

    def slots_in(k, c):
        o = lax.rem(me + k, n)
        slot_copy(o, o).wait_recv()
        return c

    lax.fori_loop(1, n, slots_in, 0)
    owned = pool.shape[0]
    ids = lax.broadcasted_iota(jnp.int32, (owned, LANES), 0) + 1
    together = LANES // cap
    for j in range(total // LANES):
        tile = slot_recv[j * together]
        for k in range(1, together):
            tile = tile + slot_recv[j * together + k]
        pool[:, j * LANES:(j + 1) * LANES] = one_hot(tile[0:1].astype(jnp.int32) == ids)

    def rows_in(k, c):
        o = lax.rem(me + k, n)
        row_copy(o, o).wait_recv()
        return c

    lax.fori_loop(1, n, rows_in, 0)
    h, l = split(recv[...].reshape(total, width))
    pooled = jnp.dot(pool[...], jnp.concatenate([h, l], axis=1), preferred_element_type=F32)
    pooled = pooled[:, :width] + pooled[:, width:]
    templates = pooled * lax.rsqrt(jnp.sum(pooled * pooled, axis=-1, keepdims=True) + 1e-06)
    enrol[p] = templates[:ET_OWN]
    probe[e] = templates[ET_OWN:]

    def enrol_copy(k):
        to = lax.rem(p + k, np_)
        return to, pltpu.make_async_remote_copy(
            src_ref=enrol.at[p], dst_ref=enrol.at[p],
            send_sem=es_sem.at[to], recv_sem=er_sem.at[p],
            device_id=(g, e, to), device_id_type=MESH,
        )

    def enrol_arrival(o):
        return pltpu.make_async_remote_copy(
            src_ref=enrol.at[o], dst_ref=enrol.at[o],
            send_sem=es_sem.at[o], recv_sem=er_sem.at[o],
            device_id=(g, e, o), device_id_type=MESH,
        )

    def probe_copy(to, source):
        return pltpu.make_async_remote_copy(
            src_ref=probe.at[source], dst_ref=probe.at[source],
            send_sem=ps_sem.at[to], recv_sem=pr_sem.at[source],
            device_id=(g, to, p), device_id_type=MESH,
        )

    for k in range(ne - 1, 0, -1):
        probe_copy(lax.rem(e + k, ne), e).start()
    for k in range(np_ - 1, 0, -1):
        enrol_copy(k)[1].start()
    for k in range(1, ne):
        o = lax.rem(e + k, ne)
        probe_copy(o, o).wait_recv()
    for k in range(1, np_):
        enrol_arrival(lax.rem(p + k, np_)).wait_recv()

    ph, pl_ = split(probe[...].reshape(ne * PT_OWN, width))
    right = jnp.concatenate([ph, ph, pl_], axis=1)
    slope, offset = scale[0], bias[0]
    for k in range(np_):
        eh, el = split(enrol[k])
        cosine = nt(jnp.concatenate([eh, el, eh], axis=1), right)
        out[k * ET_OWN:(k + 1) * ET_OWN, :] = jax.nn.sigmoid(slope * cosine + offset).astype(BF16)

    def drain(k, c):
        o = lax.rem(me + k, n)
        slot_copy(o, me).wait_send()
        row_copy(o, me).wait_send()
        return c

    lax.fori_loop(1, n, drain, 0)
    for k in range(1, ne):
        probe_copy(lax.rem(e + k, ne), e).wait_send()
    for k in range(1, np_):
        enrol_copy(k)[1].wait_send()


def shards(ne, np_, images, w_first, w_second, calib_scale, calib_bias, template_slot, media_counts):
    n = ne * np_
    here, features = images.shape
    hidden, width = w_second.shape
    cap = 2 * here // n
    total = n * cap
    chunk = 256
    chunks = hidden // chunk
    vmem = pl.BlockSpec(memory_space=pltpu.VMEM)
    smem = pl.BlockSpec(memory_space=pltpu.SMEM)
    hbm = pl.BlockSpec(memory_space=pltpu.HBM)
    dma = pltpu.SemaphoreType.DMA
    return pl.pallas_call(
        functools.partial(kernel, ne, np_, chunk),
        out_shape=jax.ShapeDtypeStruct((np_ * ET_OWN, ne * PT_OWN), BF16),
        in_specs=[hbm, hbm, hbm, smem, smem, vmem, smem],
        out_specs=vmem,
        scratch_shapes=[
            pltpu.VMEM((2, here // 2, features), F32),
            pltpu.VMEM((chunks, features, chunk), F32),
            pltpu.VMEM((chunks, chunk, width), F32),
            pltpu.VMEM((chunks, features, chunk), BF16),
            pltpu.VMEM((chunks, features, chunk), BF16),
            pltpu.VMEM((chunks, chunk, width), BF16),
            pltpu.VMEM((chunks, chunk, width), BF16),
            pltpu.VMEM((total, here), BF16),
            pltpu.VMEM((here, 2 * width), BF16),
            pltpu.VMEM((total // LANES, 8, LANES), F32),
            pltpu.VMEM((n, 8, LANES), F32),
            pltpu.VMEM((n, 8, LANES), F32),
            pltpu.VMEM((n, cap, width), F32),
            pltpu.VMEM((n, cap, width), F32),
            pltpu.VMEM((ET_OWN + PT_OWN, total), BF16),
            pltpu.VMEM((np_, ET_OWN, width), F32),
            pltpu.VMEM((ne, PT_OWN, width), F32),
            dma((2,)), dma((chunks,)), dma((chunks,)),
            dma((n,)), dma((n,)), dma((n,)), dma((n,)),
            dma((np_,)), dma((np_,)), dma((ne,)), dma((ne,)),
        ],
        compiler_params=pltpu.CompilerParams(
            collective_id=0, has_side_effects=True, vmem_limit_bytes=60 * 1024 * 1024
        ),
    )(
        images, w_first, w_second, calib_scale, calib_bias,
        template_slot.reshape(1, here), media_counts,
    )


def solution(mesh):
    ne, np_ = mesh.shape["enrol"], mesh.shape["probe"]
    return jax.shard_map(
        functools.partial(shards, ne, np_),
        mesh=mesh,
        in_specs=(
            P(("groups", "enrol", "probe"), None),
            P(),
            P(),
            P(),
            P(),
            P(("groups", "enrol", "probe")),
            P(("groups", "enrol", "probe"), None),
        ),
        out_specs=P(("groups", "enrol"), "probe"),
        check_vma=False,
    )
```
